32 devices in a mesh: groups: 2 (over y), pages: 4 (over z), heads: 4 (over x, core).
Axes of the slice: x: 2, y: 2, z: 4, core: 2. Of those that a mesh axis runs over, the one named last changes fastest.
Arguments:
- q_nope: bfloat16 [256, 16384], P(('groups', 'pages'), 'heads'), parts along dimension 0, may hold values from -6 to 6
- q_rope: bfloat16 [256, 8192], P(('groups', 'pages'), 'heads'), parts along dimension 0, may hold values from -16 to 16
- cache_tiles: bfloat16 [12288, 576], P(('groups', 'pages')), parts along dimension 0, may hold values from -8 to 8
- absorb_keys: bfloat16 [128, 128, 512], P('heads'), may hold values from -0.5 to 0.5
- absorb_values: bfloat16 [128, 512, 128], P('heads'), may hold values from -2 to 2
- page_counts: int32 [8], P('groups'), parts along dimension 0, may hold values from 1 to 24, as said below
- query_token: int32 [256], P('groups'), parts along dimension 0, may hold values from 0 to 127, each once
- query_offsets: int32 [256], P('groups'), parts along dimension 0, may hold values from 512 to 2048
Outputs:
- attention_out: bfloat16 [256, 16384], P(('groups', 'pages'), 'heads'), parts along dimension 0
The draws below stay inside these ranges and needn't reach their ends.
There are 2 independent parts, one for each index of `groups`. The reference program is written for one: setup_inputs(seed, part) draws one part's arguments, and reference() takes and returns one part's arrays. A program takes and returns all parts, laid end to end along the dimension named above; an argument that names none is the same for every part. Nothing has to cross between parts.
Inputs may be any that keep to these rules, and one draw needn't show every extreme that they name: Member m's live pages are its first page_counts[m] page slots; the counts sum to 32. `query_token`: a permutation of the span's tokens. Token t attends to the live cache rows whose key_position is below query_offsets[t].
All inputs are finite; a program needn't handle non-finite values.
Results may differ from the reference program's by a relative error of at most 0.022.
Values may be sent and summed in bfloat16 or wider, within the bound.
A program may use at most 64 MiB of HBM per device.

```python
import jax
import jax.numpy as jnp
from jax import lax

HEADS = 128
NOPE = 128
ROPE = 64
LATENT = 512
VHEAD = 128
PAGE = 64
QUERIES = 128
MEMBERS = 4
CAP = 24
TOTAL_PAGES = 32
CACHE_ROWS = 6144


def draw_page_counts(key, part):
    shuffled = jax.random.permutation(jax.random.fold_in(key, 91), MEMBERS).astype(jnp.int32)
    ranks = jnp.zeros((MEMBERS,), jnp.int32).at[shuffled].set(jnp.arange(MEMBERS, dtype=jnp.int32))
    heavy_count = max(MEMBERS // 4, 1)
    light_count = MEMBERS - heavy_count
    leftover = TOTAL_PAGES - heavy_count * CAP
    spare = leftover - light_count
    grid_slots = light_count * (CAP - 1)
    placed = jax.random.permutation(jax.random.fold_in(key, 97), grid_slots).astype(jnp.int32)
    chosen = (placed < spare).astype(jnp.int32).reshape(light_count, CAP - 1)
    light_counts = 1 + jnp.sum(chosen, axis=1).astype(jnp.int32)
    light_rank = jnp.clip(ranks - heavy_count, 0, light_count - 1)
    light_value = light_counts[light_rank]
    return jnp.where(ranks < heavy_count, jnp.int32(CAP), light_value).astype(jnp.int32)


def draw_cache_tiles(key, part):
    first = jax.random.fold_in(jax.random.fold_in(key, 31), 0)
    tiles = jnp.clip(jax.random.normal(first, (CACHE_ROWS, LATENT + ROPE), jnp.float32), -6.0, 6.0)
    return tiles.astype(jnp.bfloat16)


def draw_q_rope(key, part):
    first = jax.random.fold_in(key, 53)
    values = jnp.clip(jax.random.normal(first, (QUERIES, HEADS, ROPE), jnp.float32), -6.0, 6.0)
    return values.reshape(QUERIES, HEADS * ROPE).astype(jnp.bfloat16)


def touch_ends(entries, stream_key, smallest, high):
    longest = entries.shape.index(max(entries.shape))
    spots = []
    for shift in (0, 1):
        where = [jax.random.randint(jax.random.fold_in(stream_key, axis), (), 0, length) for axis, length in enumerate(entries.shape)]
        where[longest] = (where[longest] + shift) % entries.shape[longest]
        spots.append(tuple(where))
    return entries.at[spots[0]].set(smallest).at[spots[1]].set(high)


def block_levels(stream_key, shape, pieces, least, high):
    gain = 1.0
    for dim, parts in pieces:
        draws = jax.random.uniform(jax.random.fold_in(jax.random.fold_in(stream_key, 6), dim), (parts,), jnp.float32, least / len(pieces), high / len(pieces))
        gain = gain * jnp.repeat(jnp.exp(draws), shape[dim] // parts).reshape((-1,) + (1,) * (len(shape) - 1 - dim))
    return gain


def normal_values(key, extent, spread, most, pieces=(), held_as=jnp.bfloat16):
    entries = jax.random.normal(key, extent, jnp.float32) * spread
    if len(pieces) > 0:
        entries = block_levels(key, extent, pieces, -0.22, 0.18) * entries
    return jnp.clip(entries, min=-most, max=most).astype(held_as)


def setup_inputs(seed: int = 0, part: int = 0) -> dict:
    key_list = jax.random.split(jax.random.key(seed), 9)
    own_keys = jax.random.split(jax.random.fold_in(key_list[8], part), 9)
    return {
        "q_nope": normal_values(own_keys[0], (QUERIES, HEADS * NOPE), 1.0, 6.0, ((0, 4), (1, 4))),
        "q_rope": draw_q_rope(jax.random.fold_in(jax.random.fold_in(key_list[8], part), 71), part),
        "cache_tiles": draw_cache_tiles(jax.random.fold_in(jax.random.fold_in(key_list[8], part), 71), part),
        "absorb_keys": normal_values(key_list[3], (HEADS, NOPE, LATENT), NOPE ** -0.5, 0.5, ((0, 4),)),
        "absorb_values": normal_values(key_list[4], (HEADS, LATENT, VHEAD), 8 ** -0.5, 2.0, ((0, 4),)),
        "page_counts": draw_page_counts(jax.random.fold_in(jax.random.fold_in(key_list[8], part), 71), part),
        "query_token": jax.random.permutation(own_keys[6], QUERIES).astype(jnp.int32),
        "query_offsets": touch_ends(jax.random.randint(own_keys[7], (QUERIES,), PAGE * TOTAL_PAGES // 4, PAGE * TOTAL_PAGES + 1), jax.random.fold_in(own_keys[7], 1), PAGE * TOTAL_PAGES // 4, PAGE * TOTAL_PAGES).astype(jnp.int32),
    }


def reference(q_nope, q_rope, cache_tiles, absorb_keys, absorb_values, page_counts, query_token, query_offsets):
    slot_pages = CAP
    prefix = jnp.cumsum(page_counts) - page_counts
    slots = jnp.arange(MEMBERS * slot_pages, dtype=jnp.int32)
    member = slots // slot_pages
    within = slots % slot_pages
    live = within < page_counts[member]
    logical = prefix[member] + within
    inside = jnp.arange(PAGE, dtype=jnp.int32)
    positions = logical[:, None] * PAGE + inside[None, :]
    positions = jnp.where(live[:, None], positions, jnp.int32(2 ** 30)).reshape(-1)
    inverse = jnp.zeros((QUERIES,), jnp.int32).at[query_token].set(jnp.arange(QUERIES, dtype=jnp.int32))
    visible = positions[None, :] < query_offsets[:, None]
    group_heads = 8
    group_count = HEADS // group_heads
    nope_tok = q_nope[inverse].reshape(QUERIES, group_count, group_heads, NOPE).transpose(1, 0, 2, 3)
    rope_tok = q_rope[inverse].reshape(QUERIES, group_count, group_heads, ROPE).transpose(1, 0, 2, 3)
    keys_grouped = absorb_keys.reshape(group_count, group_heads, NOPE, LATENT)
    values_grouped = absorb_values.reshape(group_count, group_heads, LATENT, VHEAD)
    scale = (NOPE + ROPE) ** -0.5
    latent_part = cache_tiles[:, :LATENT]

    def one_group(inputs):
        nope_part, rope_part, keys_part, values_part = inputs
        q_latent = jnp.einsum("qhn,hnl->qhl", nope_part.astype(jnp.float32), keys_part.astype(jnp.float32),
                              precision=lax.Precision.HIGHEST).astype(jnp.bfloat16)
        full = jnp.concatenate([q_latent, rope_part], axis=-1).reshape(QUERIES * group_heads, LATENT + ROPE)
        scores = jnp.dot(full, cache_tiles.T, preferred_element_type=jnp.float32)
        scores = scores.reshape(QUERIES, group_heads, -1) * scale
        mask = visible[:, None, :]
        row_max = jnp.max(jnp.where(mask, scores, -jnp.inf), axis=-1, keepdims=True)
        weights = jnp.where(mask, jnp.exp(scores - row_max), 0.0)
        denominator = jnp.sum(weights, axis=-1)
        rounded = weights.astype(jnp.bfloat16).reshape(QUERIES * group_heads, -1)
        summed = jnp.dot(rounded, latent_part, preferred_element_type=jnp.float32).reshape(QUERIES, group_heads, LATENT)
        latent_out = summed / denominator[..., None]
        return jnp.einsum("qhl,hlv->qhv", latent_out, values_part.astype(jnp.float32),
                          precision=lax.Precision.HIGHEST)

    outputs = lax.map(one_group, (nope_tok, rope_tok, keys_grouped, values_grouped))
    return outputs.transpose(1, 0, 2, 3).reshape(QUERIES, HEADS * VHEAD).astype(jnp.bfloat16)
```

```python
import functools
import math

import jax
import jax.numpy as jnp
from jax import lax
from jax.experimental import pallas as pl
from jax.experimental.pallas import tpu as pltpu
from jax.sharding import PartitionSpec as P

PAGE = 64
SLOTS_PER_LIVE = 3
HEAD_BLOCK = 8
NEG = -1e30


def attend_kernel(factor, limits_ref, nope_ref, rope_ref, keys_ref, wk_ref, wv_ref, out_ref):
    block, nope_width, latent = wk_ref.shape
    rows = nope_ref.shape[0]
    value_width = wv_ref.shape[2]
    rope_width = rope_ref.shape[1] // block
    latents = []
    ropes = []
    for h in range(block):
        latents.append(
            jnp.dot(
                nope_ref[:, h * nope_width : (h + 1) * nope_width],
                wk_ref[h],
                preferred_element_type=jnp.float32,
            ).astype(jnp.bfloat16)
        )
        ropes.append(rope_ref[:, h * rope_width : (h + 1) * rope_width])
    q_latent = jnp.concatenate(latents, axis=0)
    q_rope = jnp.concatenate(ropes, axis=0)
    contract = (((1,), (1,)), ((), ()))
    scores = lax.dot_general(
        q_latent, keys_ref[:, :latent], contract, preferred_element_type=jnp.float32
    ) + lax.dot_general(
        q_rope, keys_ref[:, latent:], contract, preferred_element_type=jnp.float32
    )
    limits = jnp.concatenate([limits_ref[...]] * block, axis=0)
    position = lax.broadcasted_iota(jnp.int32, scores.shape, 1)
    scores = jnp.where(position < limits, scores, NEG)
    top = jnp.max(scores, axis=1, keepdims=True)
    weights = jnp.exp2((scores - top) * factor)
    total = jnp.sum(weights, axis=1, keepdims=True)
    mixed = jnp.dot(
        weights.astype(jnp.bfloat16), keys_ref[:, :latent], preferred_element_type=jnp.float32
    )
    mixed = (mixed / total).astype(jnp.bfloat16)
    for h in range(block):
        out_ref[:, h * value_width : (h + 1) * value_width] = jnp.dot(
            mixed[h * rows : (h + 1) * rows], wv_ref[h], preferred_element_type=jnp.float32
        ).astype(out_ref.dtype)


def attend(limits, q_nope, q_rope, keys, absorb_keys, absorb_values):
    heads, nope_width, latent = absorb_keys.shape
    value_width = absorb_values.shape[2]
    rows = q_nope.shape[0]
    rope_width = q_rope.shape[1] // heads
    block = min(HEAD_BLOCK, heads)
    factor = (nope_width + rope_width) ** (-0.5) * math.log2(math.e)
    live, full = keys.shape
    return pl.pallas_call(
        functools.partial(attend_kernel, factor),
        grid=(heads // block,),
        out_shape=jax.ShapeDtypeStruct((rows, heads * value_width), jnp.bfloat16),
        in_specs=[
            pl.BlockSpec((rows, 1), lambda i: (0, 0)),
            pl.BlockSpec((rows, block * nope_width), lambda i: (0, i)),
            pl.BlockSpec((rows, block * rope_width), lambda i: (0, i)),
            pl.BlockSpec((live, full), lambda i: (0, 0)),
            pl.BlockSpec((block, nope_width, latent), lambda i: (i, 0, 0)),
            pl.BlockSpec((block, latent, value_width), lambda i: (i, 0, 0)),
        ],
        out_specs=pl.BlockSpec((rows, block * value_width), lambda i: (0, i)),
        compiler_params=pltpu.CompilerParams(vmem_limit_bytes=56 * 2**20),
        cost_estimate=pl.CostEstimate(
            flops=2 * rows * heads * live * (full + latent),
            bytes_accessed=2 * (absorb_keys.size + absorb_values.size + keys.size),
            transcendentals=rows * heads * live,
        ),
    )(limits, q_nope, q_rope, keys, absorb_keys, absorb_values)


def own_part(cache_tiles, page_counts, members, parts):
    member = lax.axis_index("pages")
    part = lax.axis_index("heads")
    slot_rows, full = cache_tiles.shape
    live_rows = slot_rows * members // SLOTS_PER_LIVE
    length = live_rows // parts
    before = jnp.sum(jnp.where(jnp.arange(members) < member, page_counts, 0)) * PAGE
    count = jnp.sum(jnp.where(jnp.arange(members) == member, page_counts, 0)) * PAGE
    start = jnp.clip(part * length - before, -length, slot_rows)
    padded = jnp.pad(cache_tiles, ((length, length), (0, 0)))
    rows = lax.dynamic_slice(padded, (start + length, 0), (length, full))
    index = start + jnp.arange(length)
    mine = (index >= 0) & (index < count)
    return jnp.where(mine[:, None], rows, jnp.zeros((), rows.dtype))


def on_device(
    members,
    parts,
    q_nope,
    q_rope,
    cache_tiles,
    absorb_keys,
    absorb_values,
    page_counts,
    query_token,
    query_offsets,
):
    member = lax.axis_index("pages")
    rows = q_nope.shape[0]
    tokens = query_token.shape[0]
    own = own_part(cache_tiles, page_counts, members, parts)
    merged = lax.psum(own, "pages")
    keys = lax.all_gather(merged, "heads", axis=0, tiled=True)
    my_token = lax.dynamic_slice(query_token, (member * rows,), (rows,))
    limits = jnp.sum(
        jnp.where(my_token[:, None] == jnp.arange(tokens)[None, :], query_offsets[None, :], 0),
        axis=1,
        keepdims=True,
    )
    out = attend(limits, q_nope, q_rope, keys, absorb_keys, absorb_values)
    gathered = lax.all_gather(out, "pages", axis=0, tiled=True)
    wanted = member * rows + jnp.arange(rows)
    pick = (wanted[:, None] == query_token[None, :]).astype(jnp.bfloat16)
    return jnp.dot(pick, gathered, preferred_element_type=jnp.float32).astype(jnp.bfloat16)


def solution(mesh):
    in_specs = (
        P(("groups", "pages"), "heads"),
        P(("groups", "pages"), "heads"),
        P(("groups", "pages"), None),
        P("heads", None, None),
        P("heads", None, None),
        P("groups"),
        P("groups"),
        P("groups"),
    )
    out_specs = P(("groups", "pages"), "heads")
    return jax.shard_map(
        functools.partial(on_device, mesh.shape["pages"], mesh.shape["heads"]),
        mesh=mesh,
        in_specs=in_specs,
        out_specs=out_specs,
        check_vma=False,
    )
```

```python
import functools
import math

import jax
import jax.numpy as jnp
from jax import lax
from jax.experimental import pallas as pl
from jax.experimental.pallas import tpu as pltpu
from jax.sharding import PartitionSpec as P

PAGE = 64
SLOTS_PER_LIVE = 3
HEAD_BLOCK = 8
CORES = 2
MESH = pl.DeviceIdType.MESH
NEG = -1e30


def attend_kernel(factor, limits_ref, nope_ref, rope_ref, keys_ref, wk_ref, wv_ref, out_ref):
    block, nope_width, latent = wk_ref.shape
    rows = nope_ref.shape[0]
    value_width = wv_ref.shape[2]
    rope_width = rope_ref.shape[1] // block
    latents = []
    ropes = []
    for h in range(block):
        latents.append(
            jnp.dot(
                nope_ref[:, h * nope_width : (h + 1) * nope_width],
                wk_ref[h],
                preferred_element_type=jnp.float32,
            ).astype(jnp.bfloat16)
        )
        ropes.append(rope_ref[:, h * rope_width : (h + 1) * rope_width])
    q_latent = jnp.concatenate(latents, axis=0)
    q_rope = jnp.concatenate(ropes, axis=0)
    contract = (((1,), (1,)), ((), ()))
    scores = lax.dot_general(
        q_latent, keys_ref[:, :latent], contract, preferred_element_type=jnp.float32
    ) + lax.dot_general(
        q_rope, keys_ref[:, latent:], contract, preferred_element_type=jnp.float32
    )
    limits = jnp.concatenate([limits_ref[...]] * block, axis=0)
    position = lax.broadcasted_iota(jnp.int32, scores.shape, 1)
    scores = jnp.where(position < limits, scores, NEG)
    top = jnp.max(scores, axis=1, keepdims=True)
    weights = jnp.exp2((scores - top) * factor)
    total = jnp.sum(weights, axis=1, keepdims=True)
    mixed = jnp.dot(
        weights.astype(jnp.bfloat16), keys_ref[:, :latent], preferred_element_type=jnp.float32
    )
    mixed = (mixed / total).astype(jnp.bfloat16)
    for h in range(block):
        out_ref[:, h * value_width : (h + 1) * value_width] = jnp.dot(
            mixed[h * rows : (h + 1) * rows], wv_ref[h], preferred_element_type=jnp.float32
        ).astype(out_ref.dtype)


def attend(limits, q_nope, q_rope, keys, absorb_keys, absorb_values):
    heads, nope_width, latent = absorb_keys.shape
    value_width = absorb_values.shape[2]
    rows = q_nope.shape[0]
    rope_width = q_rope.shape[1] // heads
    block = min(HEAD_BLOCK, heads)
    factor = (nope_width + rope_width) ** (-0.5) * math.log2(math.e)
    live, full = keys.shape
    return pl.pallas_call(
        functools.partial(attend_kernel, factor),
        grid=(heads // block,),
        out_shape=jax.ShapeDtypeStruct((rows, heads * value_width), jnp.bfloat16),
        in_specs=[
            pl.BlockSpec((rows, 1), lambda i: (0, 0)),
            pl.BlockSpec((rows, block * nope_width), lambda i: (0, i)),
            pl.BlockSpec((rows, block * rope_width), lambda i: (0, i)),
            pl.BlockSpec((live, full), lambda i: (0, 0)),
            pl.BlockSpec((block, nope_width, latent), lambda i: (i, 0, 0)),
            pl.BlockSpec((block, latent, value_width), lambda i: (i, 0, 0)),
        ],
        out_specs=pl.BlockSpec((rows, block * value_width), lambda i: (0, i)),
        compiler_params=pltpu.CompilerParams(vmem_limit_bytes=56 * 2**20),
        cost_estimate=pl.CostEstimate(
            flops=2 * rows * heads * live * (full + latent),
            bytes_accessed=2 * (absorb_keys.size + absorb_values.size + keys.size),
            transcendentals=rows * heads * live,
        ),
    )(limits, q_nope, q_rope, keys, absorb_keys, absorb_values)


def page_kernel(place_ref, cache_ref, out_ref):
    slot = place_ref[0] + pl.program_id(0)
    live = (slot >= 0) & (slot < place_ref[1])
    out_ref[...] = jnp.where(live, cache_ref[...], jnp.zeros_like(cache_ref))


def own_part(cache_tiles, page_counts, members, parts):
    member = lax.axis_index("pages")
    part = lax.axis_index("heads")
    slot_rows, full = cache_tiles.shape
    slots = slot_rows // PAGE
    pages = slots * members // SLOTS_PER_LIVE // parts
    before = jnp.sum(jnp.where(jnp.arange(members) < member, page_counts, 0))
    count = jnp.sum(jnp.where(jnp.arange(members) == member, page_counts, 0))
    place = jnp.stack([part * pages - before, count]).astype(jnp.int32)
    return pl.pallas_call(
        page_kernel,
        grid_spec=pltpu.PrefetchScalarGridSpec(
            num_scalar_prefetch=1,
            grid=(pages,),
            in_specs=[
                pl.BlockSpec((PAGE, full), lambda i, place: (jnp.clip(place[0] + i, 0, slots - 1), 0))
            ],
            out_specs=pl.BlockSpec((PAGE, full), lambda i, place: (i, 0)),
        ),
        out_shape=jax.ShapeDtypeStruct((pages * PAGE, full), cache_tiles.dtype),
    )(place, cache_tiles)


def share_kernel(
    members, parts, own_ref, keys_ref, up_ref, down_ref, up_out, down_out,
    up_send, up_recv, down_send, down_recv, x_send, x_recv, core_send, core_recv,
):
    m = lax.axis_index("pages")
    part = lax.axis_index("heads")
    chips = parts // CORES
    chip, core = part // CORES, part % CORES
    sibling = chip * CORES + (CORES - 1 - core)
    length = own_ref.shape[0]
    chunks = length // PAGE
    last = members - 1
    has_low, has_high = m > 0, m < last

    def across(k):
        return lax.rem(chip + k, chips) * CORES + core

    barrier = pltpu.get_barrier_semaphore()

    @pl.when(has_low)
    def _():
        pl.semaphore_signal(barrier, inc=1, device_id={"pages": m - 1}, device_id_type=MESH)

    @pl.when(has_high)
    def _():
        pl.semaphore_signal(barrier, inc=1, device_id={"pages": m + 1}, device_id_type=MESH)

    for k in range(1, chips):
        pl.semaphore_signal(barrier, inc=1, device_id={"heads": across(k)}, device_id_type=MESH)
    pl.semaphore_signal(barrier, inc=1, device_id={"heads": sibling}, device_id_type=MESH)

    @pl.when(m == 0)
    def _():
        up_ref[...] = jnp.zeros_like(up_ref)

    @pl.when(m == last)
    def _():
        down_ref[...] = jnp.zeros_like(down_ref)

    pl.semaphore_wait(barrier, chips + has_low.astype(jnp.int32) + has_high.astype(jnp.int32))

    def rows(c):
        return pl.ds(pl.multiple_of(c * PAGE, PAGE), PAGE)

    def key_rows(p, c):
        return pl.ds(pl.multiple_of(p * length + c * PAGE, PAGE), PAGE)

    def up_copy(c):
        return pltpu.make_async_remote_copy(
            up_out.at[rows(c)], up_ref.at[rows(c)], up_send.at[c], up_recv.at[c],
            device_id={"pages": m + 1}, device_id_type=MESH,
        )

    def down_copy(c):
        return pltpu.make_async_remote_copy(
            down_out.at[rows(c)], down_ref.at[rows(c)], down_send.at[c], down_recv.at[c],
            device_id={"pages": m - 1}, device_id_type=MESH,
        )

    def x_copy(k, p, c):
        return pltpu.make_async_remote_copy(
            keys_ref.at[key_rows(p, c)], keys_ref.at[key_rows(p, c)],
            x_send.at[k, c], x_recv.at[k, c],
            device_id={"heads": across(k)}, device_id_type=MESH,
        )

    def core_copy(k, p, c):
        return pltpu.make_async_remote_copy(
            keys_ref.at[key_rows(p, c)], keys_ref.at[key_rows(p, c)],
            core_send.at[k, c], core_recv.at[k, c],
            device_id={"heads": sibling}, device_id_type=MESH,
        )

    late = jnp.maximum(m, last - m)

    def step(t, _):
        c_up = t - m
        c_down = t - (last - m)
        c_done = t - late
        c_next = t - late - 1

        @pl.when((c_up >= 0) & (c_up < chunks))
        def _():
            @pl.when(has_low)
            def _():
                up_copy(c_up).wait_recv()

            @pl.when(has_high)
            def _():
                up_out[rows(c_up), :] = up_ref[rows(c_up), :] + own_ref[rows(c_up), :]
                up_copy(c_up).start()

        @pl.when((c_down >= 0) & (c_down < chunks))
        def _():
            @pl.when(has_high)
            def _():
                down_copy(c_down).wait_recv()

            @pl.when(has_low)
            def _():
                down_out[rows(c_down), :] = down_ref[rows(c_down), :] + own_ref[rows(c_down), :]
                down_copy(c_down).start()

        @pl.when((c_done >= 0) & (c_done < chunks))
        def _():
            keys_ref[key_rows(part, c_done), :] = (
                up_ref[rows(c_done), :] + own_ref[rows(c_done), :] + down_ref[rows(c_done), :]
            )
            for k in range(1, chips):
                x_copy(k, part, c_done).start()
            core_copy(0, part, c_done).start()

        @pl.when((c_next >= 0) & (c_next < chunks))
        def _():
            for k in range(1, chips):
                sender = lax.rem(chip + chips - k, chips) * CORES + core
                x_copy(k, sender, c_next).wait_recv()
                core_copy(k, sender, c_next).start()

        return 0

    lax.fori_loop(0, chunks + members, step, 0)

    def finish(c, _):
        @pl.when(has_high)
        def _():
            up_copy(c).wait_send()

        @pl.when(has_low)
        def _():
            down_copy(c).wait_send()

        for k in range(chips):
            origin = lax.rem(chip + chips - k, chips) * CORES
            if k:
                x_copy(k, part, c).wait_send()
            core_copy(k, origin + core, c).wait_send()
            core_copy(k, origin + (CORES - 1 - core), c).wait_recv()
        return 0

    lax.fori_loop(0, chunks, finish, 0)


def share(own, members, parts):
    length, full = own.shape
    chunks = length // PAGE
    chips = parts // CORES
    buffer = pltpu.VMEM((length, full), own.dtype)
    line = pltpu.SemaphoreType.DMA((chunks,))
    wide = pltpu.SemaphoreType.DMA((chips, chunks))
    vmem = pl.BlockSpec(memory_space=pltpu.VMEM)
    return pl.pallas_call(
        functools.partial(share_kernel, members, parts),
        out_shape=jax.ShapeDtypeStruct((parts * length, full), own.dtype),
        in_specs=[vmem],
        out_specs=vmem,
        scratch_shapes=[buffer] * 4 + [line] * 4 + [wide] * 4,
        compiler_params=pltpu.CompilerParams(
            collective_id=0, has_side_effects=True, vmem_limit_bytes=40 * 2**20
        ),
    )(own)


def on_device(
    members,
    parts,
    q_nope,
    q_rope,
    cache_tiles,
    absorb_keys,
    absorb_values,
    page_counts,
    query_token,
    query_offsets,
):
    member = lax.axis_index("pages")
    rows = q_nope.shape[0]
    tokens = query_token.shape[0]
    own = own_part(cache_tiles, page_counts, members, parts)
    keys = share(own, members, parts)
    my_token = lax.dynamic_slice(query_token, (member * rows,), (rows,))
    limits = jnp.sum(
        jnp.where(my_token[:, None] == jnp.arange(tokens)[None, :], query_offsets[None, :], 0),
        axis=1,
        keepdims=True,
    )
    out = attend(limits, q_nope, q_rope, keys, absorb_keys, absorb_values)
    gathered = lax.all_gather(out, "pages", axis=0, tiled=True)
    wanted = member * rows + jnp.arange(rows)
    pick = (wanted[:, None] == query_token[None, :]).astype(jnp.bfloat16)
    return jnp.dot(pick, gathered, preferred_element_type=jnp.float32).astype(jnp.bfloat16)


def solution(mesh):
    in_specs = (
        P(("groups", "pages"), "heads"),
        P(("groups", "pages"), "heads"),
        P(("groups", "pages"), None),
        P("heads", None, None),
        P("heads", None, None),
        P("groups"),
        P("groups"),
        P("groups"),
    )
    out_specs = P(("groups", "pages"), "heads")
    return jax.shard_map(
        functools.partial(on_device, mesh.shape["pages"], mesh.shape["heads"]),
        mesh=mesh,
        in_specs=in_specs,
        out_specs=out_specs,
        check_vma=False,
    )
```

```python
import functools
import math

import jax
import jax.numpy as jnp
from jax import lax
from jax.experimental import pallas as pl
from jax.experimental.pallas import tpu as pltpu
from jax.sharding import PartitionSpec as P

PAGE = 64
SLOTS_PER_LIVE = 3
HEAD_BLOCK = 8
CORES = 2
CHUNK = 128
MESH = pl.DeviceIdType.MESH
NEG = -1e30


def attend_kernel(factor, limits_ref, nope_ref, rope_ref, keys_ref, wk_ref, wv_ref, out_ref):
    block, nope_width, latent = wk_ref.shape
    rows = nope_ref.shape[0]
    value_width = wv_ref.shape[2]
    rope_width = rope_ref.shape[1] // block
    latents = []
    ropes = []
    for h in range(block):
        latents.append(
            jnp.dot(
                nope_ref[:, h * nope_width : (h + 1) * nope_width],
                wk_ref[h],
                preferred_element_type=jnp.float32,
            ).astype(jnp.bfloat16)
        )
        ropes.append(rope_ref[:, h * rope_width : (h + 1) * rope_width])
    q_latent = jnp.concatenate(latents, axis=0)
    q_rope = jnp.concatenate(ropes, axis=0)
    contract = (((1,), (1,)), ((), ()))
    scores = lax.dot_general(
        q_latent, keys_ref[:, :latent], contract, preferred_element_type=jnp.float32
    ) + lax.dot_general(
        q_rope, keys_ref[:, latent:], contract, preferred_element_type=jnp.float32
    )
    limits = jnp.concatenate([limits_ref[...]] * block, axis=0)
    position = lax.broadcasted_iota(jnp.int32, scores.shape, 1)
    scores = jnp.where(position < limits, scores, NEG)
    top = jnp.max(scores, axis=1, keepdims=True)
    weights = jnp.exp2((scores - top) * factor)
    total = jnp.sum(weights, axis=1, keepdims=True)
    mixed = jnp.dot(
        weights.astype(jnp.bfloat16), keys_ref[:, :latent], preferred_element_type=jnp.float32
    )
    mixed = (mixed / total).astype(jnp.bfloat16)
    for h in range(block):
        out_ref[:, h * value_width : (h + 1) * value_width] = jnp.dot(
            mixed[h * rows : (h + 1) * rows], wv_ref[h], preferred_element_type=jnp.float32
        ).astype(out_ref.dtype)


def attend(limits, q_nope, q_rope, keys, absorb_keys, absorb_values):
    heads, nope_width, latent = absorb_keys.shape
    value_width = absorb_values.shape[2]
    rows = q_nope.shape[0]
    rope_width = q_rope.shape[1] // heads
    block = min(HEAD_BLOCK, heads)
    factor = (nope_width + rope_width) ** (-0.5) * math.log2(math.e)
    live, full = keys.shape
    return pl.pallas_call(
        functools.partial(attend_kernel, factor),
        grid=(heads // block,),
        out_shape=jax.ShapeDtypeStruct((rows, heads * value_width), jnp.bfloat16),
        in_specs=[
            pl.BlockSpec((rows, 1), lambda i: (0, 0)),
            pl.BlockSpec((rows, block * nope_width), lambda i: (0, i)),
            pl.BlockSpec((rows, block * rope_width), lambda i: (0, i)),
            pl.BlockSpec((live, full), lambda i: (0, 0)),
            pl.BlockSpec((block, nope_width, latent), lambda i: (i, 0, 0)),
            pl.BlockSpec((block, latent, value_width), lambda i: (i, 0, 0)),
        ],
        out_specs=pl.BlockSpec((rows, block * value_width), lambda i: (0, i)),
        compiler_params=pltpu.CompilerParams(vmem_limit_bytes=56 * 2**20),
        cost_estimate=pl.CostEstimate(
            flops=2 * rows * heads * live * (full + latent),
            bytes_accessed=2 * (absorb_keys.size + absorb_values.size + keys.size),
            transcendentals=rows * heads * live,
        ),
    )(limits, q_nope, q_rope, keys, absorb_keys, absorb_values)


def page_kernel(members, parts, counts_ref, cache_ref, out_ref, sems):
    member = lax.axis_index("pages")
    slots = cache_ref.shape[0] // PAGE
    pages = out_ref.shape[0] // PAGE
    before = lax.fori_loop(0, member, lambda j, total: total + counts_ref[j], jnp.int32(0))
    count = counts_ref[member]
    first = lax.axis_index("heads") * pages - before

    def page(j):
        slot = jnp.clip(first + j, 0, slots - 1)
        return pltpu.make_async_copy(
            cache_ref.at[pl.ds(pl.multiple_of(slot * PAGE, PAGE), PAGE)],
            out_ref.at[pl.ds(j * PAGE, PAGE)],
            sems.at[j],
        )

    for j in range(pages):
        page(j).start()
    for j in range(pages):
        page(j).wait()

        @pl.when((first + j < 0) | (first + j >= count))
        def _():
            out_ref[pl.ds(j * PAGE, PAGE), :] = jnp.zeros((PAGE, out_ref.shape[1]), out_ref.dtype)


def own_part(cache_tiles, page_counts, members, parts):
    slot_rows, full = cache_tiles.shape
    pages = slot_rows // PAGE * members // SLOTS_PER_LIVE // parts
    return pl.pallas_call(
        functools.partial(page_kernel, members, parts),
        in_specs=[
            pl.BlockSpec(memory_space=pltpu.SMEM),
            pl.BlockSpec(memory_space=pl.ANY),
        ],
        out_specs=pl.BlockSpec(memory_space=pltpu.VMEM),
        out_shape=jax.ShapeDtypeStruct((pages * PAGE, full), cache_tiles.dtype),
        scratch_shapes=[pltpu.SemaphoreType.DMA((pages,))],
    )(page_counts, cache_tiles)


def share_kernel(
    members, parts, own_ref, keys_ref, up_ref, down_ref, up_out, down_out,
    up_send, up_recv, down_send, down_recv, x_send, x_recv, core_send, core_recv,
):
    m = lax.axis_index("pages")
    part = lax.axis_index("heads")
    chips = parts // CORES
    chip, core = part // CORES, part % CORES
    sibling = chip * CORES + (CORES - 1 - core)
    length = own_ref.shape[0]
    chunks = length // CHUNK
    last = members - 1
    has_low, has_high = m > 0, m < last

    def across(k):
        return lax.rem(chip + k, chips) * CORES + core

    barrier = pltpu.get_barrier_semaphore()

    @pl.when(has_low)
    def _():
        pl.semaphore_signal(barrier, inc=1, device_id={"pages": m - 1}, device_id_type=MESH)

    @pl.when(has_high)
    def _():
        pl.semaphore_signal(barrier, inc=1, device_id={"pages": m + 1}, device_id_type=MESH)

    for k in range(1, chips):
        pl.semaphore_signal(barrier, inc=1, device_id={"heads": across(k)}, device_id_type=MESH)
    pl.semaphore_signal(barrier, inc=1, device_id={"heads": sibling}, device_id_type=MESH)

    @pl.when(m == 0)
    def _():
        up_ref[...] = jnp.zeros_like(up_ref)

    @pl.when(m == last)
    def _():
        down_ref[...] = jnp.zeros_like(down_ref)

    pl.semaphore_wait(barrier, chips + has_low.astype(jnp.int32) + has_high.astype(jnp.int32))

    def rows(c):
        return pl.ds(pl.multiple_of(c * CHUNK, CHUNK), CHUNK)

    def key_rows(p, c):
        return pl.ds(pl.multiple_of(p * length + c * CHUNK, CHUNK), CHUNK)

    def up_copy(c):
        return pltpu.make_async_remote_copy(
            up_out.at[rows(c)], up_ref.at[rows(c)], up_send.at[c], up_recv.at[c],
            device_id={"pages": m + 1}, device_id_type=MESH,
        )

    def down_copy(c):
        return pltpu.make_async_remote_copy(
            down_out.at[rows(c)], down_ref.at[rows(c)], down_send.at[c], down_recv.at[c],
            device_id={"pages": m - 1}, device_id_type=MESH,
        )

    def x_copy(k, p, c):
        return pltpu.make_async_remote_copy(
            keys_ref.at[key_rows(p, c)], keys_ref.at[key_rows(p, c)],
            x_send.at[k, c], x_recv.at[k, c],
            device_id={"heads": across(k)}, device_id_type=MESH,
        )

    def core_copy(k, p, c):
        return pltpu.make_async_remote_copy(
            keys_ref.at[key_rows(p, c)], keys_ref.at[key_rows(p, c)],
            core_send.at[k, c], core_recv.at[k, c],
            device_id={"heads": sibling}, device_id_type=MESH,
        )

    late = jnp.maximum(m, last - m)

    def step(t, _):
        c_up = t - m
        c_down = t - (last - m)
        c_done = t - late
        c_next = t - late - 1

        @pl.when((c_up >= 0) & (c_up < chunks))
        def _():
            @pl.when(has_low)
            def _():
                up_copy(c_up).wait_recv()

            @pl.when(has_high)
            def _():
                up_out[rows(c_up), :] = up_ref[rows(c_up), :] + own_ref[rows(c_up), :]
                up_copy(c_up).start()

        @pl.when((c_down >= 0) & (c_down < chunks))
        def _():
            @pl.when(has_high)
            def _():
                down_copy(c_down).wait_recv()

            @pl.when(has_low)
            def _():
                down_out[rows(c_down), :] = down_ref[rows(c_down), :] + own_ref[rows(c_down), :]
                down_copy(c_down).start()

        @pl.when((c_done >= 0) & (c_done < chunks))
        def _():
            keys_ref[key_rows(part, c_done), :] = (
                up_ref[rows(c_done), :] + own_ref[rows(c_done), :] + down_ref[rows(c_done), :]
            )
            for k in range(1, chips):
                x_copy(k, part, c_done).start()
            core_copy(0, part, c_done).start()

        @pl.when((c_next >= 0) & (c_next < chunks))
        def _():
            for k in range(1, chips):
                sender = lax.rem(chip + chips - k, chips) * CORES + core
                x_copy(k, sender, c_next).wait_recv()
                core_copy(k, sender, c_next).start()

        return 0

    lax.fori_loop(0, chunks + members, step, 0)

    def finish(c, _):
        @pl.when(has_high)
        def _():
            up_copy(c).wait_send()

        @pl.when(has_low)
        def _():
            down_copy(c).wait_send()

        for k in range(chips):
            origin = lax.rem(chip + chips - k, chips) * CORES
            if k:
                x_copy(k, part, c).wait_send()
            core_copy(k, origin + core, c).wait_send()
            core_copy(k, origin + (CORES - 1 - core), c).wait_recv()
        return 0

    lax.fori_loop(0, chunks, finish, 0)


def share(own, members, parts):
    length, full = own.shape
    chunks = length // CHUNK
    chips = parts // CORES
    buffer = pltpu.VMEM((length, full), own.dtype)
    line = pltpu.SemaphoreType.DMA((chunks,))
    wide = pltpu.SemaphoreType.DMA((chips, chunks))
    vmem = pl.BlockSpec(memory_space=pltpu.VMEM)
    return pl.pallas_call(
        functools.partial(share_kernel, members, parts),
        out_shape=jax.ShapeDtypeStruct((parts * length, full), own.dtype),
        in_specs=[vmem],
        out_specs=vmem,
        scratch_shapes=[buffer] * 4 + [line] * 4 + [wide] * 4,
        compiler_params=pltpu.CompilerParams(
            collective_id=0, has_side_effects=True, vmem_limit_bytes=40 * 2**20
        ),
    )(own)


def on_device(
    members,
    parts,
    q_nope,
    q_rope,
    cache_tiles,
    absorb_keys,
    absorb_values,
    page_counts,
    query_token,
    query_offsets,
):
    member = lax.axis_index("pages")
    rows = q_nope.shape[0]
    tokens = query_token.shape[0]
    own = own_part(cache_tiles, page_counts, members, parts)
    keys = share(own, members, parts)
    my_token = lax.dynamic_slice(query_token, (member * rows,), (rows,))
    limits = jnp.sum(
        jnp.where(my_token[:, None] == jnp.arange(tokens)[None, :], query_offsets[None, :], 0),
        axis=1,
        keepdims=True,
    )
    out = attend(limits, q_nope, q_rope, keys, absorb_keys, absorb_values)
    gathered = lax.all_gather(out, "pages", axis=0, tiled=True)
    wanted = member * rows + jnp.arange(rows)
    pick = (wanted[:, None] == query_token[None, :]).astype(jnp.bfloat16)
    return jnp.dot(pick, gathered, preferred_element_type=jnp.float32).astype(jnp.bfloat16)


def solution(mesh):
    in_specs = (
        P(("groups", "pages"), "heads"),
        P(("groups", "pages"), "heads"),
        P(("groups", "pages"), None),
        P("heads", None, None),
        P("heads", None, None),
        P("groups"),
        P("groups"),
        P("groups"),
    )
    out_specs = P(("groups", "pages"), "heads")
    return jax.shard_map(
        functools.partial(on_device, mesh.shape["pages"], mesh.shape["heads"]),
        mesh=mesh,
        in_specs=in_specs,
        out_specs=out_specs,
        check_vma=False,
    )
```

```python
import functools
import math

import jax
import jax.numpy as jnp
from jax import lax
from jax.experimental import pallas as pl
from jax.experimental.pallas import tpu as pltpu
from jax.sharding import PartitionSpec as P

PAGE = 64
SLOTS_PER_LIVE = 3
HEAD_BLOCK = 8
CORES = 2
CHUNK = 128
MESH = pl.DeviceIdType.MESH
NEG = -1e30


def attend_kernel(
    factor, members, blocks, limits_ref, token_ref, nope_ref, rope_ref, keys_ref, wk_ref, wv_ref, out_ref,
    held, up_send, up_recv, down_send, down_recv,
):
    m = lax.axis_index("pages")
    last = members - 1
    now = pl.program_id(0)

    @pl.when(now == 0)
    def _():
        barrier = pltpu.get_barrier_semaphore()
        for there, step in ((m > 0, -1), (m < last, 1)):

            @pl.when(there)
            def _(step=step):
                pl.semaphore_signal(barrier, inc=1, device_id={"pages": m + step}, device_id_type=MESH)

        pl.semaphore_wait(barrier, (m > 0).astype(jnp.int32) + (m < last).astype(jnp.int32))

    block, nope_width, latent = wk_ref.shape
    rows = nope_ref.shape[0]
    value_width = wv_ref.shape[2]
    rope_width = rope_ref.shape[1] // block
    latents = []
    ropes = []
    for h in range(block):
        latents.append(
            jnp.dot(
                nope_ref[:, h * nope_width : (h + 1) * nope_width],
                wk_ref[h],
                preferred_element_type=jnp.float32,
            ).astype(jnp.bfloat16)
        )
        ropes.append(rope_ref[:, h * rope_width : (h + 1) * rope_width])
    q_latent = jnp.concatenate(latents, axis=0)
    q_rope = jnp.concatenate(ropes, axis=0)
    contract = (((1,), (1,)), ((), ()))
    scores = lax.dot_general(
        q_latent, keys_ref[:, :latent], contract, preferred_element_type=jnp.float32
    ) + lax.dot_general(
        q_rope, keys_ref[:, latent:], contract, preferred_element_type=jnp.float32
    )
    limits = jnp.concatenate([limits_ref[...]] * block, axis=0)
    position = lax.broadcasted_iota(jnp.int32, scores.shape, 1)
    scores = jnp.where(position < limits, scores, NEG)
    top = jnp.max(scores, axis=1, keepdims=True)
    weights = jnp.exp2((scores - top) * factor)
    total = jnp.sum(weights, axis=1, keepdims=True)
    mixed = jnp.dot(
        weights.astype(jnp.bfloat16), keys_ref[:, :latent], preferred_element_type=jnp.float32
    )
    mixed = (mixed / total).astype(jnp.bfloat16)
    mine = pl.ds(pl.multiple_of(m * rows, rows), rows)
    for h in range(block):
        held[now, mine, h * value_width : (h + 1) * value_width] = jnp.dot(
            mixed[h * rows : (h + 1) * rows], wv_ref[h], preferred_element_type=jnp.float32
        ).astype(held.dtype)

    def hop(origin, d, b, step, send, recv):
        part = held.at[b, pl.ds(pl.multiple_of(origin * rows, rows), rows)]
        return pltpu.make_async_remote_copy(
            part, part, send.at[d, b], recv.at[d, b],
            device_id={"pages": m + step}, device_id_type=MESH,
        )

    ways = ((1, up_send, up_recv), (-1, down_send, down_recv))

    def tick(t):
        def distance(d, _):
            b = t - d
            for step, send, recv in ways:
                origin = m - step * d
                there = (b >= 0) & (b < blocks) & (origin >= 0) & (origin <= last)

                @pl.when(there & (d > 0))
                def _(step=step, send=send, recv=recv, origin=origin):
                    hop(origin, d - 1, b, step, send, recv).wait_recv()

                @pl.when(there & (m + step >= 0) & (m + step <= last))
                def _(step=step, send=send, recv=recv, origin=origin):
                    hop(origin, d, b, step, send, recv).start()

            return 0

        lax.fori_loop(0, members, distance, 0)

    tick(now)

    @pl.when(now == blocks - 1)
    def _():
        lax.fori_loop(blocks, blocks + last, lambda t, _: (tick(t), 0)[1], 0)

        def sent(i, _):
            d, b = i // blocks, i % blocks
            for step, send, recv in ways:
                origin = m - step * d
                there = (origin >= 0) & (origin <= last) & (m + step >= 0) & (m + step <= last)

                @pl.when(there)
                def _(step=step, send=send, recv=recv, origin=origin):
                    hop(origin, d, b, step, send, recv).wait_send()

            return 0

        lax.fori_loop(0, members * blocks, sent, 0)
        tokens = held.shape[1]
        wanted = m * rows + lax.broadcasted_iota(jnp.int32, (rows, tokens), 0)
        pick = (wanted == token_ref[...]).astype(jnp.bfloat16)
        wide = block * value_width
        for b in range(blocks):
            out_ref[:, b * wide : (b + 1) * wide] = jnp.dot(
                pick, held[b], preferred_element_type=jnp.float32
            ).astype(out_ref.dtype)


def attend(members, limits, query_token, q_nope, q_rope, keys, absorb_keys, absorb_values):
    heads, nope_width, latent = absorb_keys.shape
    value_width = absorb_values.shape[2]
    rows = q_nope.shape[0]
    rope_width = q_rope.shape[1] // heads
    block = min(HEAD_BLOCK, heads)
    factor = (nope_width + rope_width) ** (-0.5) * math.log2(math.e)
    live, full = keys.shape
    return pl.pallas_call(
        functools.partial(attend_kernel, factor, members, heads // block),
        grid=(heads // block,),
        out_shape=jax.ShapeDtypeStruct((rows, heads * value_width), jnp.bfloat16),
        in_specs=[
            pl.BlockSpec((rows, 1), lambda i: (0, 0)),
            pl.BlockSpec((1, members * rows), lambda i: (0, 0)),
            pl.BlockSpec((rows, block * nope_width), lambda i: (0, i)),
            pl.BlockSpec((rows, block * rope_width), lambda i: (0, i)),
            pl.BlockSpec((live, full), lambda i: (0, 0)),
            pl.BlockSpec((block, nope_width, latent), lambda i: (i, 0, 0)),
            pl.BlockSpec((block, latent, value_width), lambda i: (i, 0, 0)),
        ],
        out_specs=pl.BlockSpec((rows, heads * value_width), lambda i: (0, 0)),
        scratch_shapes=[
            pltpu.VMEM((heads // block, members * rows, block * value_width), jnp.bfloat16)
        ]
        + [pltpu.SemaphoreType.DMA((members, heads // block))] * 4,
        compiler_params=pltpu.CompilerParams(
            collective_id=1, has_side_effects=True, vmem_limit_bytes=56 * 2**20
        ),
        cost_estimate=pl.CostEstimate(
            flops=2 * rows * heads * live * (full + latent),
            bytes_accessed=2 * (absorb_keys.size + absorb_values.size + keys.size),
            transcendentals=rows * heads * live,
        ),
    )(limits, query_token[None, :], q_nope, q_rope, keys, absorb_keys, absorb_values)


def page_kernel(members, parts, counts_ref, cache_ref, out_ref, sems):
    member = lax.axis_index("pages")
    slots = cache_ref.shape[0] // PAGE
    pages = out_ref.shape[0] // PAGE
    before = lax.fori_loop(0, member, lambda j, total: total + counts_ref[j], jnp.int32(0))
    count = counts_ref[member]
    first = lax.axis_index("heads") * pages - before

    def page(j):
        slot = jnp.clip(first + j, 0, slots - 1)
        return pltpu.make_async_copy(
            cache_ref.at[pl.ds(pl.multiple_of(slot * PAGE, PAGE), PAGE)],
            out_ref.at[pl.ds(j * PAGE, PAGE)],
            sems.at[j],
        )

    for j in range(pages):
        page(j).start()
    for j in range(pages):
        page(j).wait()

        @pl.when((first + j < 0) | (first + j >= count))
        def _():
            out_ref[pl.ds(j * PAGE, PAGE), :] = jnp.zeros((PAGE, out_ref.shape[1]), out_ref.dtype)


def own_part(cache_tiles, page_counts, members, parts):
    slot_rows, full = cache_tiles.shape
    pages = slot_rows // PAGE * members // SLOTS_PER_LIVE // parts
    return pl.pallas_call(
        functools.partial(page_kernel, members, parts),
        in_specs=[
            pl.BlockSpec(memory_space=pltpu.SMEM),
            pl.BlockSpec(memory_space=pl.ANY),
        ],
        out_specs=pl.BlockSpec(memory_space=pltpu.VMEM),
        out_shape=jax.ShapeDtypeStruct((pages * PAGE, full), cache_tiles.dtype),
        scratch_shapes=[pltpu.SemaphoreType.DMA((pages,))],
    )(page_counts, cache_tiles)


def share_kernel(
    members, parts, own_ref, keys_ref, up_ref, down_ref, up_out, down_out,
    up_send, up_recv, down_send, down_recv, x_send, x_recv, core_send, core_recv,
):
    m = lax.axis_index("pages")
    part = lax.axis_index("heads")
    chips = parts // CORES
    chip, core = part // CORES, part % CORES
    sibling = chip * CORES + (CORES - 1 - core)
    length = own_ref.shape[0]
    chunks = length // CHUNK
    last = members - 1
    has_low, has_high = m > 0, m < last

    def across(k):
        return lax.rem(chip + k, chips) * CORES + core

    barrier = pltpu.get_barrier_semaphore()

    @pl.when(has_low)
    def _():
        pl.semaphore_signal(barrier, inc=1, device_id={"pages": m - 1}, device_id_type=MESH)

    @pl.when(has_high)
    def _():
        pl.semaphore_signal(barrier, inc=1, device_id={"pages": m + 1}, device_id_type=MESH)

    for k in range(1, chips):
        pl.semaphore_signal(barrier, inc=1, device_id={"heads": across(k)}, device_id_type=MESH)
    pl.semaphore_signal(barrier, inc=1, device_id={"heads": sibling}, device_id_type=MESH)

    @pl.when(m == 0)
    def _():
        up_ref[...] = jnp.zeros_like(up_ref)

    @pl.when(m == last)
    def _():
        down_ref[...] = jnp.zeros_like(down_ref)

    pl.semaphore_wait(barrier, chips + has_low.astype(jnp.int32) + has_high.astype(jnp.int32))

    def rows(c):
        return pl.ds(pl.multiple_of(c * CHUNK, CHUNK), CHUNK)

    def key_rows(p, c):
        return pl.ds(pl.multiple_of(p * length + c * CHUNK, CHUNK), CHUNK)

    def up_copy(c):
        return pltpu.make_async_remote_copy(
            up_out.at[rows(c)], up_ref.at[rows(c)], up_send.at[c], up_recv.at[c],
            device_id={"pages": m + 1}, device_id_type=MESH,
        )

    def down_copy(c):
        return pltpu.make_async_remote_copy(
            down_out.at[rows(c)], down_ref.at[rows(c)], down_send.at[c], down_recv.at[c],
            device_id={"pages": m - 1}, device_id_type=MESH,
        )

    def x_copy(k, p, c):
        return pltpu.make_async_remote_copy(
            keys_ref.at[key_rows(p, c)], keys_ref.at[key_rows(p, c)],
            x_send.at[k, c], x_recv.at[k, c],
            device_id={"heads": across(k)}, device_id_type=MESH,
        )

    def core_copy(k, p, c):
        return pltpu.make_async_remote_copy(
            keys_ref.at[key_rows(p, c)], keys_ref.at[key_rows(p, c)],
            core_send.at[k, c], core_recv.at[k, c],
            device_id={"heads": sibling}, device_id_type=MESH,
        )

    late = jnp.maximum(m, last - m)

    def step(t, _):
        c_up = t - m
        c_down = t - (last - m)
        c_done = t - late
        c_next = t - late - 1

        @pl.when((c_up >= 0) & (c_up < chunks))
        def _():
            @pl.when(has_low)
            def _():
                up_copy(c_up).wait_recv()

            @pl.when(has_high)
            def _():
                up_out[rows(c_up), :] = up_ref[rows(c_up), :] + own_ref[rows(c_up), :]
                up_copy(c_up).start()

        @pl.when((c_down >= 0) & (c_down < chunks))
        def _():
            @pl.when(has_high)
            def _():
                down_copy(c_down).wait_recv()

            @pl.when(has_low)
            def _():
                down_out[rows(c_down), :] = down_ref[rows(c_down), :] + own_ref[rows(c_down), :]
                down_copy(c_down).start()

        @pl.when((c_done >= 0) & (c_done < chunks))
        def _():
            keys_ref[key_rows(part, c_done), :] = (
                up_ref[rows(c_done), :] + own_ref[rows(c_done), :] + down_ref[rows(c_done), :]
            )
            for k in range(1, chips):
                x_copy(k, part, c_done).start()
            core_copy(0, part, c_done).start()

        @pl.when((c_next >= 0) & (c_next < chunks))
        def _():
            for k in range(1, chips):
                sender = lax.rem(chip + chips - k, chips) * CORES + core
                x_copy(k, sender, c_next).wait_recv()
                core_copy(k, sender, c_next).start()

        return 0

    lax.fori_loop(0, chunks + members, step, 0)

    def finish(c, _):
        @pl.when(has_high)
        def _():
            up_copy(c).wait_send()

        @pl.when(has_low)
        def _():
            down_copy(c).wait_send()

        for k in range(chips):
            origin = lax.rem(chip + chips - k, chips) * CORES
            if k:
                x_copy(k, part, c).wait_send()
            core_copy(k, origin + core, c).wait_send()
            core_copy(k, origin + (CORES - 1 - core), c).wait_recv()
        return 0

    lax.fori_loop(0, chunks, finish, 0)


def share(own, members, parts):
    length, full = own.shape
    chunks = length // CHUNK
    chips = parts // CORES
    buffer = pltpu.VMEM((length, full), own.dtype)
    line = pltpu.SemaphoreType.DMA((chunks,))
    wide = pltpu.SemaphoreType.DMA((chips, chunks))
    vmem = pl.BlockSpec(memory_space=pltpu.VMEM)
    return pl.pallas_call(
        functools.partial(share_kernel, members, parts),
        out_shape=jax.ShapeDtypeStruct((parts * length, full), own.dtype),
        in_specs=[vmem],
        out_specs=vmem,
        scratch_shapes=[buffer] * 4 + [line] * 4 + [wide] * 4,
        compiler_params=pltpu.CompilerParams(
            collective_id=0, has_side_effects=True, vmem_limit_bytes=40 * 2**20
        ),
    )(own)


def on_device(
    members,
    parts,
    q_nope,
    q_rope,
    cache_tiles,
    absorb_keys,
    absorb_values,
    page_counts,
    query_token,
    query_offsets,
):
    member = lax.axis_index("pages")
    rows = q_nope.shape[0]
    tokens = query_token.shape[0]
    own = own_part(cache_tiles, page_counts, members, parts)
    keys = share(own, members, parts)
    my_token = lax.dynamic_slice(query_token, (member * rows,), (rows,))
    limits = jnp.sum(
        jnp.where(my_token[:, None] == jnp.arange(tokens)[None, :], query_offsets[None, :], 0),
        axis=1,
        keepdims=True,
    )
    return attend(
        members, limits, query_token, q_nope, q_rope, keys, absorb_keys, absorb_values
    )


def solution(mesh):
    in_specs = (
        P(("groups", "pages"), "heads"),
        P(("groups", "pages"), "heads"),
        P(("groups", "pages"), None),
        P("heads", None, None),
        P("heads", None, None),
        P("groups"),
        P("groups"),
        P("groups"),
    )
    out_specs = P(("groups", "pages"), "heads")
    return jax.shard_map(
        functools.partial(on_device, mesh.shape["pages"], mesh.shape["heads"]),
        mesh=mesh,
        in_specs=in_specs,
        out_specs=out_specs,
        check_vma=False,
    )
```

```python
import functools
import math

import jax
import jax.numpy as jnp
from jax import lax
from jax.experimental import pallas as pl
from jax.experimental.pallas import tpu as pltpu
from jax.sharding import PartitionSpec as P

PAGE = 64
SLOTS_PER_LIVE = 3
HEAD_BLOCK = 8
CORES = 2
CHUNK = 128
MESH = pl.DeviceIdType.MESH
NEG = -1e30


def attend_kernel(
    factor, members, blocks, offset_ref, token_ref, nope_ref, rope_ref, keys_ref, wk_ref, wv_ref, out_ref,
    held, up_send, up_recv, down_send, down_recv,
):
    m = lax.axis_index("pages")
    last = members - 1
    now = pl.program_id(0)

    @pl.when(now == 0)
    def _():
        barrier = pltpu.get_barrier_semaphore()
        for there, step in ((m > 0, -1), (m < last, 1)):

            @pl.when(there)
            def _(step=step):
                pl.semaphore_signal(barrier, inc=1, device_id={"pages": m + step}, device_id_type=MESH)

        pl.semaphore_wait(barrier, (m > 0).astype(jnp.int32) + (m < last).astype(jnp.int32))

    block, nope_width, latent = wk_ref.shape
    rows = nope_ref.shape[0]
    value_width = wv_ref.shape[2]
    rope_width = rope_ref.shape[1] // block
    latents = []
    ropes = []
    for h in range(block):
        latents.append(
            jnp.dot(
                nope_ref[:, h * nope_width : (h + 1) * nope_width],
                wk_ref[h],
                preferred_element_type=jnp.float32,
            ).astype(jnp.bfloat16)
        )
        ropes.append(rope_ref[:, h * rope_width : (h + 1) * rope_width])
    q_latent = jnp.concatenate(latents, axis=0)
    q_rope = jnp.concatenate(ropes, axis=0)
    contract = (((1,), (1,)), ((), ()))
    scores = lax.dot_general(
        q_latent, keys_ref[:, :latent], contract, preferred_element_type=jnp.float32
    ) + lax.dot_general(
        q_rope, keys_ref[:, latent:], contract, preferred_element_type=jnp.float32
    )
    square = (rows, token_ref.shape[1])
    lane = lax.broadcasted_iota(jnp.int32, square, 1)
    here = lane == m * rows + lax.broadcasted_iota(jnp.int32, square, 0)
    token = jnp.sum(
        jnp.where(here, token_ref[...].astype(jnp.float32), 0.0), axis=1, keepdims=True
    )
    limit = jnp.sum(
        jnp.where(lane.astype(jnp.float32) == token, offset_ref[...].astype(jnp.float32), 0.0),
        axis=1,
        keepdims=True,
    ).astype(jnp.int32)
    limits = jnp.concatenate([limit] * block, axis=0)
    position = lax.broadcasted_iota(jnp.int32, scores.shape, 1)
    scores = jnp.where(position < limits, scores, NEG)
    top = jnp.max(scores, axis=1, keepdims=True)
    weights = jnp.exp2((scores - top) * factor)
    total = jnp.sum(weights, axis=1, keepdims=True)
    mixed = jnp.dot(
        weights.astype(jnp.bfloat16), keys_ref[:, :latent], preferred_element_type=jnp.float32
    )
    mixed = (mixed / total).astype(jnp.bfloat16)
    mine = pl.ds(pl.multiple_of(m * rows, rows), rows)
    for h in range(block):
        held[now, mine, h * value_width : (h + 1) * value_width] = jnp.dot(
            mixed[h * rows : (h + 1) * rows], wv_ref[h], preferred_element_type=jnp.float32
        ).astype(held.dtype)

    def hop(origin, d, b, step, send, recv):
        part = held.at[b, pl.ds(pl.multiple_of(origin * rows, rows), rows)]
        return pltpu.make_async_remote_copy(
            part, part, send.at[d, b], recv.at[d, b],
            device_id={"pages": m + step}, device_id_type=MESH,
        )

    ways = ((1, up_send, up_recv), (-1, down_send, down_recv))

    def tick(t):
        def distance(d, _):
            b = t - d
            for step, send, recv in ways:
                origin = m - step * d
                there = (b >= 0) & (b < blocks) & (origin >= 0) & (origin <= last)

                @pl.when(there & (d > 0))
                def _(step=step, send=send, recv=recv, origin=origin):
                    hop(origin, d - 1, b, step, send, recv).wait_recv()

                @pl.when(there & (m + step >= 0) & (m + step <= last))
                def _(step=step, send=send, recv=recv, origin=origin):
                    hop(origin, d, b, step, send, recv).start()

            return 0

        lax.fori_loop(0, members, distance, 0)

    tick(now)

    @pl.when(now == blocks - 1)
    def _():
        lax.fori_loop(blocks, blocks + last, lambda t, _: (tick(t), 0)[1], 0)

        def sent(i, _):
            d, b = i // blocks, i % blocks
            for step, send, recv in ways:
                origin = m - step * d
                there = (origin >= 0) & (origin <= last) & (m + step >= 0) & (m + step <= last)

                @pl.when(there)
                def _(step=step, send=send, recv=recv, origin=origin):
                    hop(origin, d, b, step, send, recv).wait_send()

            return 0

        lax.fori_loop(0, members * blocks, sent, 0)
        tokens = held.shape[1]
        wanted = m * rows + lax.broadcasted_iota(jnp.int32, (rows, tokens), 0)
        pick = (wanted == token_ref[...]).astype(jnp.bfloat16)
        wide = block * value_width
        for b in range(blocks):
            out_ref[:, b * wide : (b + 1) * wide] = jnp.dot(
                pick, held[b], preferred_element_type=jnp.float32
            ).astype(out_ref.dtype)


def attend(members, query_offsets, query_token, q_nope, q_rope, keys, absorb_keys, absorb_values):
    heads, nope_width, latent = absorb_keys.shape
    value_width = absorb_values.shape[2]
    rows = q_nope.shape[0]
    rope_width = q_rope.shape[1] // heads
    block = min(HEAD_BLOCK, heads)
    factor = (nope_width + rope_width) ** (-0.5) * math.log2(math.e)
    live, full = keys.shape
    return pl.pallas_call(
        functools.partial(attend_kernel, factor, members, heads // block),
        grid=(heads // block,),
        out_shape=jax.ShapeDtypeStruct((rows, heads * value_width), jnp.bfloat16),
        in_specs=[
            pl.BlockSpec((1, members * rows), lambda i: (0, 0)),
            pl.BlockSpec((1, members * rows), lambda i: (0, 0)),
            pl.BlockSpec((rows, block * nope_width), lambda i: (0, i)),
            pl.BlockSpec((rows, block * rope_width), lambda i: (0, i)),
            pl.BlockSpec((live, full), lambda i: (0, 0)),
            pl.BlockSpec((block, nope_width, latent), lambda i: (i, 0, 0)),
            pl.BlockSpec((block, latent, value_width), lambda i: (i, 0, 0)),
        ],
        out_specs=pl.BlockSpec((rows, heads * value_width), lambda i: (0, 0)),
        scratch_shapes=[
            pltpu.VMEM((heads // block, members * rows, block * value_width), jnp.bfloat16)
        ]
        + [pltpu.SemaphoreType.DMA((members, heads // block))] * 4,
        compiler_params=pltpu.CompilerParams(
            collective_id=1, has_side_effects=True, vmem_limit_bytes=56 * 2**20
        ),
        cost_estimate=pl.CostEstimate(
            flops=2 * rows * heads * live * (full + latent),
            bytes_accessed=2 * (absorb_keys.size + absorb_values.size + keys.size),
            transcendentals=rows * heads * live,
        ),
    )(query_offsets[None, :], query_token[None, :], q_nope, q_rope, keys, absorb_keys, absorb_values)


def page_kernel(members, parts, counts_ref, cache_ref, out_ref, sems):
    member = lax.axis_index("pages")
    slots = cache_ref.shape[0] // PAGE
    pages = out_ref.shape[0] // PAGE
    before = lax.fori_loop(0, member, lambda j, total: total + counts_ref[j], jnp.int32(0))
    count = counts_ref[member]
    first = lax.axis_index("heads") * pages - before

    def page(j):
        slot = jnp.clip(first + j, 0, slots - 1)
        return pltpu.make_async_copy(
            cache_ref.at[pl.ds(pl.multiple_of(slot * PAGE, PAGE), PAGE)],
            out_ref.at[pl.ds(j * PAGE, PAGE)],
            sems.at[j],
        )

    for j in range(pages):
        page(j).start()
    for j in range(pages):
        page(j).wait()

        @pl.when((first + j < 0) | (first + j >= count))
        def _():
            out_ref[pl.ds(j * PAGE, PAGE), :] = jnp.zeros((PAGE, out_ref.shape[1]), out_ref.dtype)


def own_part(cache_tiles, page_counts, members, parts):
    slot_rows, full = cache_tiles.shape
    pages = slot_rows // PAGE * members // SLOTS_PER_LIVE // parts
    return pl.pallas_call(
        functools.partial(page_kernel, members, parts),
        in_specs=[
            pl.BlockSpec(memory_space=pltpu.SMEM),
            pl.BlockSpec(memory_space=pl.ANY),
        ],
        out_specs=pl.BlockSpec(memory_space=pltpu.VMEM),
        out_shape=jax.ShapeDtypeStruct((pages * PAGE, full), cache_tiles.dtype),
        scratch_shapes=[pltpu.SemaphoreType.DMA((pages,))],
    )(page_counts, cache_tiles)


def share_kernel(
    members, parts, own_ref, keys_ref, up_ref, down_ref, up_out, down_out,
    up_send, up_recv, down_send, down_recv, x_send, x_recv, core_send, core_recv,
):
    m = lax.axis_index("pages")
    part = lax.axis_index("heads")
    chips = parts // CORES
    chip, core = part // CORES, part % CORES
    sibling = chip * CORES + (CORES - 1 - core)
    length = own_ref.shape[0]
    chunks = length // CHUNK
    last = members - 1
    has_low, has_high = m > 0, m < last

    def across(k):
        return lax.rem(chip + k, chips) * CORES + core

    barrier = pltpu.get_barrier_semaphore()

    @pl.when(has_low)
    def _():
        pl.semaphore_signal(barrier, inc=1, device_id={"pages": m - 1}, device_id_type=MESH)

    @pl.when(has_high)
    def _():
        pl.semaphore_signal(barrier, inc=1, device_id={"pages": m + 1}, device_id_type=MESH)

    for k in range(1, chips):
        pl.semaphore_signal(barrier, inc=1, device_id={"heads": across(k)}, device_id_type=MESH)
    pl.semaphore_signal(barrier, inc=1, device_id={"heads": sibling}, device_id_type=MESH)

    @pl.when(m == 0)
    def _():
        up_ref[...] = jnp.zeros_like(up_ref)

    @pl.when(m == last)
    def _():
        down_ref[...] = jnp.zeros_like(down_ref)

    pl.semaphore_wait(barrier, chips + has_low.astype(jnp.int32) + has_high.astype(jnp.int32))

    def rows(c):
        return pl.ds(pl.multiple_of(c * CHUNK, CHUNK), CHUNK)

    def key_rows(p, c):
        return pl.ds(pl.multiple_of(p * length + c * CHUNK, CHUNK), CHUNK)

    def up_copy(c):
        return pltpu.make_async_remote_copy(
            up_out.at[rows(c)], up_ref.at[rows(c)], up_send.at[c], up_recv.at[c],
            device_id={"pages": m + 1}, device_id_type=MESH,
        )

    def down_copy(c):
        return pltpu.make_async_remote_copy(
            down_out.at[rows(c)], down_ref.at[rows(c)], down_send.at[c], down_recv.at[c],
            device_id={"pages": m - 1}, device_id_type=MESH,
        )

    def x_copy(k, p, c):
        return pltpu.make_async_remote_copy(
            keys_ref.at[key_rows(p, c)], keys_ref.at[key_rows(p, c)],
            x_send.at[k, c], x_recv.at[k, c],
            device_id={"heads": across(k)}, device_id_type=MESH,
        )

    def core_copy(k, p, c):
        return pltpu.make_async_remote_copy(
            keys_ref.at[key_rows(p, c)], keys_ref.at[key_rows(p, c)],
            core_send.at[k, c], core_recv.at[k, c],
            device_id={"heads": sibling}, device_id_type=MESH,
        )

    late = jnp.maximum(m, last - m)

    def step(t, _):
        c_up = t - m
        c_down = t - (last - m)
        c_done = t - late
        c_next = t - late - 1

        @pl.when((c_up >= 0) & (c_up < chunks))
        def _():
            @pl.when(has_low)
            def _():
                up_copy(c_up).wait_recv()

            @pl.when(has_high)
            def _():
                up_out[rows(c_up), :] = up_ref[rows(c_up), :] + own_ref[rows(c_up), :]
                up_copy(c_up).start()

        @pl.when((c_down >= 0) & (c_down < chunks))
        def _():
            @pl.when(has_high)
            def _():
                down_copy(c_down).wait_recv()

            @pl.when(has_low)
            def _():
                down_out[rows(c_down), :] = down_ref[rows(c_down), :] + own_ref[rows(c_down), :]
                down_copy(c_down).start()

        @pl.when((c_done >= 0) & (c_done < chunks))
        def _():
            keys_ref[key_rows(part, c_done), :] = (
                up_ref[rows(c_done), :] + own_ref[rows(c_done), :] + down_ref[rows(c_done), :]
            )
            for k in range(1, chips):
                x_copy(k, part, c_done).start()
            core_copy(0, part, c_done).start()

        @pl.when((c_next >= 0) & (c_next < chunks))
        def _():
            for k in range(1, chips):
                sender = lax.rem(chip + chips - k, chips) * CORES + core
                x_copy(k, sender, c_next).wait_recv()
                core_copy(k, sender, c_next).start()

        return 0

    lax.fori_loop(0, chunks + members, step, 0)

    def finish(c, _):
        @pl.when(has_high)
        def _():
            up_copy(c).wait_send()

        @pl.when(has_low)
        def _():
            down_copy(c).wait_send()

        for k in range(chips):
            origin = lax.rem(chip + chips - k, chips) * CORES
            if k:
                x_copy(k, part, c).wait_send()
            core_copy(k, origin + core, c).wait_send()
            core_copy(k, origin + (CORES - 1 - core), c).wait_recv()
        return 0

    lax.fori_loop(0, chunks, finish, 0)


def share(own, members, parts):
    length, full = own.shape
    chunks = length // CHUNK
    chips = parts // CORES
    buffer = pltpu.VMEM((length, full), own.dtype)
    line = pltpu.SemaphoreType.DMA((chunks,))
    wide = pltpu.SemaphoreType.DMA((chips, chunks))
    vmem = pl.BlockSpec(memory_space=pltpu.VMEM)
    return pl.pallas_call(
        functools.partial(share_kernel, members, parts),
        out_shape=jax.ShapeDtypeStruct((parts * length, full), own.dtype),
        in_specs=[vmem],
        out_specs=vmem,
        scratch_shapes=[buffer] * 4 + [line] * 4 + [wide] * 4,
        compiler_params=pltpu.CompilerParams(
            collective_id=0, has_side_effects=True, vmem_limit_bytes=40 * 2**20
        ),
    )(own)


def on_device(
    members,
    parts,
    q_nope,
    q_rope,
    cache_tiles,
    absorb_keys,
    absorb_values,
    page_counts,
    query_token,
    query_offsets,
):
    own = own_part(cache_tiles, page_counts, members, parts)
    keys = share(own, members, parts)
    return attend(
        members, query_offsets, query_token, q_nope, q_rope, keys, absorb_keys, absorb_values
    )


def solution(mesh):
    in_specs = (
        P(("groups", "pages"), "heads"),
        P(("groups", "pages"), "heads"),
        P(("groups", "pages"), None),
        P("heads", None, None),
        P("heads", None, None),
        P("groups"),
        P("groups"),
        P("groups"),
    )
    out_specs = P(("groups", "pages"), "heads")
    return jax.shard_map(
        functools.partial(on_device, mesh.shape["pages"], mesh.shape["heads"]),
        mesh=mesh,
        in_specs=in_specs,
        out_specs=out_specs,
        check_vma=False,
    )
```
